512 devices in a mesh: row: 16 (over x_hi, y, core), col: 32 (over z, x_lo).
Axes of the slice: x: 4 (x_hi: 2, x_lo: 2; x = x_hi * 2 + x_lo), y: 4, z: 16, core: 2. Of those that a mesh axis runs over, the one named last changes fastest.
Arguments:
- embeddings: bfloat16 [32768, 256], P(('row', 'col')), may hold values from -1 to 1, as said below
- prior_scores: bfloat16 [32768, 128], P(('row', 'col')), may hold values from -6 to 6
- seed_labels: int32 [32768], P(('row', 'col')), may hold values from 0 to 255
- tile_pattern: int32 [32, 32], P('row', 'col'), may hold values from 0 to 1, as said below
Outputs:
- label_scores: float32 [32768, 128], P(('row', 'col'))
The draws below stay inside these ranges and needn't reach their ends.
Inputs may be any that keep to these rules, and one draw needn't show every extreme that they name: `embeddings`: each row has length one up to bfloat16 rounding. `tile_pattern`: symmetric; every tile on the diagonal is kept; counts of kept tiles differ from row block to row block. `seed_labels`: a value of 128 or more marks a node without a seed.
All inputs are finite; a program needn't handle non-finite values.
Results may differ from the reference program's by a relative error of at most 0.006.
Values may be sent and summed in bfloat16 or wider, within the bound.
No kernel may reach another device: no remote copies, remote signals or barrier semaphores. Data moves between devices by JAX's collectives and lax.ppermute only.
A program may use at most 64 MiB of HBM per device.

```python
import jax
import jax.numpy as jnp
from jax import lax

TILE = 1024
EMB = 256
CLASSES = 128
ITERS = 2
TILES = 32
NODES = 32768


def draw_embeddings(key, part):
    key = jax.random.fold_in(key, 3)
    key_shared, key_coarse, key_jitter, key_axes = jax.random.split(key, 4)
    coarse_count = EMB // 4
    shared = jax.random.normal(key_shared, (EMB,), jnp.float32)
    shared = shared / jnp.sqrt(jnp.sum(shared * shared))
    chosen = jax.random.permutation(key_axes, EMB)
    axis_mask = (chosen < coarse_count).astype(jnp.float32)
    coarse = jax.random.normal(key_coarse, (NODES, EMB), jnp.float32)
    jitter = jax.random.normal(key_jitter, (NODES, EMB), jnp.float32)
    coarse_weight = 0.55
    coarse_full = coarse * axis_mask[None, :]
    vectors = shared[None, :] + coarse_weight / coarse_count ** 0.5 * coarse_full + 0.3 / EMB ** 0.5 * jitter
    vectors = vectors / jnp.sqrt(jnp.sum(vectors * vectors, axis=1, keepdims=True))
    return vectors.astype(jnp.bfloat16)


def draw_tile_pattern(key, part):
    key_pair, key_density = jax.random.split(jax.random.fold_in(key, 7), 2)
    jitter = jax.random.randint(key_pair, (TILES, TILES), 0, 100)
    paired = jitter + jitter.T
    density = jax.random.randint(key_density, (TILES,), 10, 90)
    limits = density[:, None] + density[None, :]
    tile_ids = jnp.arange(TILES, dtype=jnp.int32)
    diagonal = tile_ids[:, None] == tile_ids[None, :]
    return jnp.where(jnp.logical_or(paired < limits, diagonal), 1, 0).astype(jnp.int32)


def touch_ends(result, own_key, low, high):
    dims = result.shape
    spot = [jax.random.randint(jax.random.fold_in(own_key, axis), (), 0, dims[axis]) for axis in range(len(dims))]
    result = result.at[tuple(spot)].set(low)
    longest = dims.index(max(dims))
    spot[longest] = (spot[longest] + 1) % dims[longest]
    return result.at[tuple(spot)].set(high)


def block_levels(key, dims, pieces, smallest, high):
    def one(position, blocks):
        steps = jax.random.uniform(jax.random.fold_in(jax.random.fold_in(key, 6), position), (blocks,), jnp.float32, smallest / len(pieces), high / len(pieces))
        return jnp.repeat(jnp.exp(steps), dims[position] // blocks).reshape((-1,) + (1,) * (len(dims) - position - 1))

    loudness = one(*pieces[0])
    for cut in pieces[1:]:
        loudness = loudness * one(*cut)
    return loudness


def noise(own_key, shape, spread, limit, cuts=(), held_as=jnp.bfloat16):
    drawn = jax.random.normal(own_key, shape, jnp.float32) * spread
    if len(cuts) > 0:
        drawn = block_levels(own_key, shape, cuts, -0.22, 0.18) * drawn
    return jnp.clip(drawn, min=-limit, max=limit).astype(held_as)


def setup_inputs(seed: int = 0) -> dict:
    streams_of = jax.random.split(jax.random.key(seed), 5)
    return {
        "embeddings": draw_embeddings(jax.random.fold_in(streams_of[4], 71), 0),
        "prior_scores": noise(streams_of[1], (NODES, CLASSES), 1.0, 6.0, ((0, 512),)),
        "seed_labels": touch_ends(jax.random.randint(streams_of[2], (NODES,), 0, 2 * CLASSES), jax.random.fold_in(streams_of[2], 1), 0, (2 * CLASSES) - 1).astype(jnp.int32),
        "tile_pattern": draw_tile_pattern(jax.random.fold_in(streams_of[4], 71), 0),
    }


KERNEL_SPREAD = 0.05
PROPAGATE_WEIGHT = 0.9
SEED_WEIGHT = 0.1

def tile_kernel(embeddings, row_block_part, column_block_part):
    left_rows = lax.dynamic_slice_in_dim(embeddings, row_block_part * TILE, TILE, 0)
    right_rows = lax.dynamic_slice_in_dim(embeddings, column_block_part * TILE, TILE, 0)
    label_weights = jnp.dot(left_rows, right_rows.T, preferred_element_type=jnp.float32)
    return jnp.exp((label_weights - 1.0) / KERNEL_SPREAD).astype(jnp.bfloat16)

def reference(embeddings, prior_scores, seed_labels, tile_pattern):
    tile_ids = jnp.arange(TILES, dtype=jnp.int32)

    def row_degree(row_block_part):

        def add_one(column_block_part, total):
            value = lax.cond(tile_pattern[row_block_part, column_block_part] > 0, lambda: lax.optimization_barrier(jnp.sum(tile_kernel(embeddings, row_block_part, column_block_part), axis=1, dtype=jnp.float32)), lambda: jnp.zeros((TILE,), jnp.float32))
            return total + value
        return lax.fori_loop(0, TILES, add_one, jnp.zeros((TILE,), jnp.float32))
    degree = lax.map(row_degree, tile_ids).reshape(-1)
    inv_degree = 1.0 / jnp.sqrt(degree)

    def propagate(normalized_rows):

        def row_product(row_block_part):

            def add_one(column_block_part, total):
                block = lax.dynamic_slice_in_dim(normalized_rows, column_block_part * TILE, TILE, 0)
                value = lax.cond(tile_pattern[row_block_part, column_block_part] > 0, lambda: jnp.dot(tile_kernel(embeddings, row_block_part, column_block_part), block, preferred_element_type=jnp.float32), lambda: jnp.zeros((TILE, CLASSES), jnp.float32))
                return total + value
            return lax.fori_loop(0, TILES, add_one, jnp.zeros((TILE, CLASSES), jnp.float32))
        return lax.map(row_product, tile_ids).reshape(NODES, CLASSES)
    classes_iota = jnp.arange(CLASSES, dtype=jnp.int32)
    seeds = (seed_labels[:, None] == classes_iota[None, :]).astype(jnp.float32)
    present_label_weights = prior_scores.astype(jnp.float32)
    for sweep in range(ITERS):
        normalized_rows = (inv_degree[:, None] * present_label_weights).astype(jnp.bfloat16)
        product = propagate(normalized_rows)
        present_label_weights = PROPAGATE_WEIGHT * inv_degree[:, None] * product + SEED_WEIGHT * seeds
    return present_label_weights
```

```python
import jax
import jax.numpy as jnp
from jax import lax
from jax.sharding import Mesh, PartitionSpec as P

KERNEL_SPREAD = 0.05
PROPAGATE_WEIGHT = 0.9
SEED_WEIGHT = 0.1

AXES = ("xh", "y", "core", "z", "xl")
SIZES = (2, 4, 2, 16, 2)
ROW = ("xh", "y", "core")
COL = ("z", "xl")
PLANE = ("xh", "y", "xl")
LANES = 128


def spread_gather(x, axes, count):
    copies = jnp.broadcast_to(x[None], (count,) + x.shape)
    return lax.all_to_all(copies, axes, 0, 0, tiled=True)


def per_device(embeddings, prior_scores, seed_labels, tile_pattern):
    bf, f32 = jnp.bfloat16, jnp.float32
    nodes, classes = prior_scores.shape
    z = lax.axis_index("z")
    z_half = z // 8
    halves = [embeddings[:, :LANES], embeddings[:, LANES:]]
    pattern = tile_pattern.astype(bf)

    flags = jnp.broadcast_to(jnp.repeat(pattern[:, 0], LANES // 2)[None, :], (8, LANES))
    panel = spread_gather(jnp.concatenate(halves + [flags], 0), PLANE, 16)
    panel = lax.all_gather(panel, "core", axis=0)
    emb_b = jnp.concatenate([panel[:, :, :nodes], panel[:, :, nodes : 2 * nodes]], 3)
    emb_b = emb_b.reshape(32 * nodes, 2 * LANES)
    flags = panel[:, :, 2 * nodes, :: LANES // 2].reshape(2, 2, 4, 2, 2)
    flags = flags[lax.axis_index("core"), lax.axis_index("xh"), lax.axis_index("y")]

    flags = jnp.broadcast_to(flags.reshape(4, 1), (4, LANES))
    flags = jnp.concatenate([flags, flags], 0)
    column = lax.all_gather(jnp.concatenate(halves + [prior_scores, flags], 0), "z", axis=0)
    emb_a = jnp.concatenate([column[:, :nodes], column[:, nodes : 2 * nodes]], 2)
    emb_a = emb_a.reshape(16 * nodes, 2 * LANES)
    prior_a = column[:, 2 * nodes : 3 * nodes].reshape(16 * nodes, classes)
    kept = column[:, 3 * nodes : 3 * nodes + 4, 0].reshape(16, 2, 2)
    kept = lax.dynamic_index_in_dim(kept, z_half, 1, False)
    kept = kept.reshape(2, 4, 2, 2).transpose(2, 0, 1, 3).reshape(16, 2)

    weights = lax.dot_general(emb_b, emb_a, (((1,), (1,)), ((), ())), preferred_element_type=f32)
    kernel = jnp.exp((weights - 1.0) / KERNEL_SPREAD)
    keep = jnp.broadcast_to(kept[:, None, :, None], (16, 2 * nodes, 2, 8 * nodes))
    kernel = jnp.where(keep.reshape(kernel.shape) > 0, kernel, 0.0).astype(bf)

    partial = jnp.sum(kernel, axis=0, dtype=f32).reshape(8, LANES)
    degree = jnp.sum(spread_gather(partial, "z", 16), axis=0).reshape(16, nodes)
    inv = 1.0 / jnp.sqrt(degree)
    inv_own = lax.dynamic_index_in_dim(inv, z, 0, False)[:, None]
    inv = inv.reshape(-1, 1)
    classes_iota = jnp.arange(classes, dtype=jnp.int32)
    seeds = SEED_WEIGHT * (seed_labels[:, None] == classes_iota[None, :]).astype(f32)

    scaled_a = (inv * prior_a.astype(f32)).astype(bf)
    part = jnp.dot(kernel, scaled_a, preferred_element_type=f32).astype(bf)
    part = lax.all_to_all(part.reshape(32, nodes, classes), ("core",) + PLANE, 0, 0, tiled=True)
    product = jnp.sum(part.astype(f32), axis=0)
    scores = PROPAGATE_WEIGHT * inv_own * product + seeds

    scaled = (inv_own * scores).astype(bf)
    scaled_b = lax.all_gather(spread_gather(scaled, PLANE, 16), "core", axis=0)
    scaled_b = scaled_b.reshape(32 * nodes, classes)
    part = lax.dot_general(kernel, scaled_b, (((0,), (0,)), ((), ())), preferred_element_type=f32)
    part = lax.all_to_all(part.astype(bf).reshape(16, nodes, classes), "z", 0, 0, tiled=True)
    product = jnp.sum(part.astype(f32), axis=0)
    return PROPAGATE_WEIGHT * inv_own * product + seeds


def solution(mesh):
    return jax.shard_map(
        per_device,
        mesh=Mesh(mesh.devices.reshape(SIZES), AXES),
        in_specs=(P(AXES, None), P(AXES, None), P(AXES), P(ROW, COL)),
        out_specs=P(AXES, None),
        check_vma=False,
    )
```

```python
import functools

import jax
import jax.numpy as jnp
from jax import lax
from jax.experimental import pallas as pl
from jax.experimental.pallas import tpu as pltpu
from jax.sharding import Mesh, PartitionSpec as P

KERNEL_SPREAD = 0.05
PROPAGATE_WEIGHT = 0.9
SEED_WEIGHT = 0.1
RATE = 1.4426950408889634 / KERNEL_SPREAD
DROPPED = -1.0e30

AXES = ("xh", "y", "core", "z", "xl")
SIZES = (2, 4, 2, 16, 2)
ROW = ("xh", "y", "core")
COL = ("z", "xl")
PLANE = ("xh", "y", "xl")
LANES = 128
N = 64
A = 16 * N
H = 16 * N
BF = jnp.bfloat16
F32 = jnp.float32
PARAMS = pltpu.CompilerParams(vmem_limit_bytes=40 * 1024 * 1024)


def spread_gather(x, axes, count):
    copies = jnp.broadcast_to(x[None], (count,) + x.shape)
    return lax.all_to_all(copies, axes, 0, 0, tiled=True)


def similarity_kernel(column_ref, panel_ref, offset_ref, kernel_ref, sums_ref):
    for j in range(4):
        lo = panel_ref[4 * j : 4 * j + 4, :N, :].reshape(4 * N, LANES)
        hi = panel_ref[4 * j : 4 * j + 4, N : 2 * N, :].reshape(4 * N, LANES)
        right = jnp.concatenate([lo, hi], 1)
        sums = jnp.zeros((1, 4 * N), F32)
        for a in range(2):
            offset = jnp.concatenate(
                [offset_ref[a, 2 * j : 2 * j + 1, :], offset_ref[a, 2 * j + 1 : 2 * j + 2, :]], 1
            )
            for q in range(2):
                rows = 4 * (2 * a + q)
                lo = column_ref[rows : rows + 4, :N, :].reshape(4 * N, LANES)
                hi = column_ref[rows : rows + 4, N : 2 * N, :].reshape(4 * N, LANES)
                left = jnp.concatenate([lo, hi], 1)
                weights = lax.dot_general(
                    left, right, (((1,), (1,)), ((), ())), preferred_element_type=F32
                )
                tile = jnp.exp2(weights * RATE + offset).astype(BF)
                kernel_ref[rows * N : (rows + 4) * N, 4 * j * N : 4 * (j + 1) * N] = tile
                sums = sums + jnp.sum(tile.astype(F32), axis=0, keepdims=True)
        sums_ref[2 * j : 2 * j + 1, :] = sums[:, :LANES]
        sums_ref[2 * j + 1 : 2 * j + 2, :] = sums[:, LANES:]


def similarity(column, panel, offset):
    return pl.pallas_call(
        similarity_kernel,
        out_shape=(jax.ShapeDtypeStruct((A, H), BF), jax.ShapeDtypeStruct((8, LANES), F32)),
        compiler_params=PARAMS,
        cost_estimate=pl.CostEstimate(
            flops=2 * A * H * 256, bytes_accessed=4 << 20, transcendentals=A * H
        ),
        name="similarity",
    )(column, panel, offset)


def first_kernel(core_ref, parts_ref, prior0_ref, prior1_ref, k0_ref, k1_ref, out_ref, inv_ref):
    core = core_ref[0]
    total = None
    for side, (prior_ref, k_ref) in enumerate(((prior0_ref, k0_ref), (prior1_ref, k1_ref))):
        at = core if side == 0 else 1 - core
        inv = 1.0 / jnp.sqrt(jnp.sum(parts_ref[:, at], axis=0))
        inv_ref[at] = inv
        turned = inv.T
        scaled = []
        for k in range(8):
            prior = prior_ref[2 * k : 2 * k + 2].reshape(2 * N, LANES).astype(F32)
            scaled.append((turned[:, k : k + 1] * prior).astype(BF))
        scaled = jnp.concatenate(scaled, 0)
        part = jnp.dot(k_ref[...], scaled, preferred_element_type=F32)
        total = part if total is None else total + part
    out_ref[...] = total.astype(BF)


def first_product(core, parts, panel0, panel1, k0, k1):
    whole = lambda *shape: pl.BlockSpec(shape, lambda i: (0,) * len(shape))
    prior = pl.BlockSpec((16, N, LANES), lambda i: (0, 2, 0))
    return pl.pallas_call(
        first_kernel,
        grid=(1,),
        in_specs=[
            pl.BlockSpec(memory_space=pltpu.SMEM),
            whole(32, 2, 8, LANES),
            prior,
            prior,
            whole(A, H),
            whole(A, H),
        ],
        out_specs=(whole(A, LANES), whole(2, 8, LANES)),
        out_shape=(
            jax.ShapeDtypeStruct((A, LANES), BF),
            jax.ShapeDtypeStruct((2, 8, LANES), F32),
        ),
        compiler_params=PARAMS,
        cost_estimate=pl.CostEstimate(
            flops=4 * A * H * LANES, bytes_accessed=5 << 20, transcendentals=0
        ),
        name="first_product",
    )(core, parts, panel0, panel1, k0, k1)


def second_kernel(core_ref, scaled_ref, k0_ref, k1_ref, out_ref):
    core = core_ref[0]
    total = jnp.dot(k0_ref[...], scaled_ref[core].reshape(H, LANES), preferred_element_type=F32)
    total += jnp.dot(k1_ref[...], scaled_ref[1 - core].reshape(H, LANES), preferred_element_type=F32)
    out_ref[...] = total.astype(BF)


def second_product(core, scaled, k0, k1):
    vmem = pl.BlockSpec(memory_space=pltpu.VMEM)
    return pl.pallas_call(
        second_kernel,
        in_specs=[pl.BlockSpec(memory_space=pltpu.SMEM), vmem, vmem, vmem],
        out_shape=jax.ShapeDtypeStruct((A, LANES), BF),
        compiler_params=PARAMS,
        cost_estimate=pl.CostEstimate(
            flops=4 * A * H * LANES, bytes_accessed=5 << 20, transcendentals=0
        ),
        name="second_product",
    )(core, scaled, k0, k1)


def per_device(embeddings, prior_scores, seed_labels, tile_pattern):
    z, core = lax.axis_index("z"), lax.axis_index("core")
    halves = [embeddings[:, :LANES], embeddings[:, LANES:]]

    panel0 = spread_gather(jnp.concatenate(halves + [prior_scores], 0), PLANE, 16)

    flags = jnp.repeat(tile_pattern[:, 0].astype(BF), LANES // 2)
    flags = lax.all_gather(jnp.broadcast_to(flags[None, :], (8, LANES)), "xl", axis=0, tiled=True)
    column = lax.all_gather(jnp.concatenate(halves + [flags], 0), "z", axis=0)
    kept = column[:, 2 * N :: 8, :: LANES // 2]
    kept = lax.dynamic_index_in_dim(kept, z // 8, 1, False)
    offset = jnp.where(kept > 0, -RATE, DROPPED).astype(F32).reshape(8, 2, 2)
    offset = jnp.broadcast_to(offset.transpose(1, 2, 0)[..., None], (2, 2, 8, LANES))

    panel1 = lax.ppermute(panel0, "core", [(0, 1), (1, 0)])
    take = functools.partial(lax.dynamic_index_in_dim, axis=0, keepdims=False)
    kernel0, sums0 = similarity(column, panel0, take(offset, core))
    kernel1, sums1 = similarity(column, panel1, take(offset, 1 - core))

    sums = jnp.where(core == 0, jnp.stack([sums0, sums1]), jnp.stack([sums1, sums0]))
    parts = spread_gather(sums, ("core",) + PLANE, 32)
    core_word = core.astype(jnp.int32).reshape(1)
    part, inv = first_product(core_word, parts.reshape(32, 2, 8, LANES), panel0, panel1, kernel0, kernel1)
    inv_own = take(inv.reshape(32, N), lax.axis_index(("core",) + PLANE))[:, None]
    classes_iota = jnp.arange(LANES, dtype=jnp.int32)
    seeds = SEED_WEIGHT * (seed_labels[:, None] == classes_iota[None, :]).astype(F32)

    part = lax.all_to_all(part.reshape(16, N, LANES), "z", 0, 0, tiled=True)
    product = jnp.sum(part.astype(F32), axis=0)
    scores = PROPAGATE_WEIGHT * inv_own * product + seeds

    scaled = spread_gather((inv_own * scores).astype(BF), PLANE, 16)
    scaled = lax.all_gather(scaled, "core", axis=0)
    part = second_product(core_word, scaled, kernel0, kernel1)
    part = lax.all_to_all(part.reshape(16, N, LANES), "z", 0, 0, tiled=True)
    product = jnp.sum(part.astype(F32), axis=0)
    return PROPAGATE_WEIGHT * inv_own * product + seeds


def solution(mesh):
    return jax.shard_map(
        per_device,
        mesh=Mesh(mesh.devices.reshape(SIZES), AXES),
        in_specs=(P(AXES, None), P(AXES, None), P(AXES), P(ROW, COL)),
        out_specs=P(AXES, None),
        check_vma=False,
    )
```

```python
import jax
import jax.numpy as jnp
from jax import lax
from jax.experimental import pallas as pl
from jax.experimental.pallas import tpu as pltpu
from jax.sharding import Mesh, PartitionSpec as P

KERNEL_SPREAD = 0.05
PROPAGATE_WEIGHT = 0.9
SEED_WEIGHT = 0.1
RATE = 1.4426950408889634 / KERNEL_SPREAD
DROPPED = -1.0e30

AXES = ("xh", "y", "core", "z", "xl")
SIZES = (2, 4, 2, 16, 2)
ROW = ("xh", "y", "core")
COL = ("z", "xl")
LANES = 128
N = 64
A = 16 * N
B = 32 * N
PLANE = ("core", "xh", "y", "xl")
BF = jnp.bfloat16
F32 = jnp.float32
PARAMS = pltpu.CompilerParams(vmem_limit_bytes=24 * 1024 * 1024)


def spread_gather(x, axes, count):
    copies = jnp.broadcast_to(x[None], (count,) + x.shape)
    return lax.all_to_all(copies, axes, 0, 0, tiled=True)


def similarity_kernel(column_ref, panel_ref, offset_ref, kernel_ref, sums_ref):
    for j in range(8):
        lo = panel_ref[4 * j : 4 * j + 4, :N, :].reshape(4 * N, LANES)
        hi = panel_ref[4 * j : 4 * j + 4, N : 2 * N, :].reshape(4 * N, LANES)
        right = jnp.concatenate([lo, hi], 1)
        sums = jnp.zeros((1, 4 * N), F32)
        for a in range(2):
            offset = jnp.concatenate(
                [offset_ref[a, 2 * j : 2 * j + 1, :], offset_ref[a, 2 * j + 1 : 2 * j + 2, :]], 1
            )
            for q in range(2):
                rows = 4 * (2 * a + q)
                lo = column_ref[rows : rows + 4, :N, :].reshape(4 * N, LANES)
                hi = column_ref[rows : rows + 4, N : 2 * N, :].reshape(4 * N, LANES)
                left = jnp.concatenate([lo, hi], 1)
                weights = lax.dot_general(
                    left, right, (((1,), (1,)), ((), ())), preferred_element_type=F32
                )
                tile = jnp.exp2(weights * RATE + offset).astype(BF)
                kernel_ref[rows * N : (rows + 4) * N, 4 * j * N : 4 * (j + 1) * N] = tile
                sums = sums + jnp.sum(tile.astype(F32), axis=0, keepdims=True)
        sums_ref[2 * j : 2 * j + 1, :] = sums[:, :LANES]
        sums_ref[2 * j + 1 : 2 * j + 2, :] = sums[:, LANES:]


def similarity(column, panel, offset):
    return pl.pallas_call(
        similarity_kernel,
        out_shape=(jax.ShapeDtypeStruct((A, B), BF), jax.ShapeDtypeStruct((16, LANES), F32)),
        compiler_params=PARAMS,
        cost_estimate=pl.CostEstimate(
            flops=2 * A * B * 256, bytes_accessed=4 << 20, transcendentals=A * B
        ),
        name="similarity",
    )(column, panel, offset)


def first_kernel(parts_ref, panel_ref, kernel_ref, out_ref, inv_ref):
    inv = 1.0 / jnp.sqrt(jnp.sum(parts_ref[...], axis=0))
    inv_ref[...] = inv
    turned = inv.T
    scaled = []
    for k in range(16):
        prior = panel_ref[2 * k : 2 * k + 2, 2 * N : 3 * N, :].reshape(2 * N, LANES).astype(F32)
        scaled.append((turned[:, k : k + 1] * prior).astype(BF))
    scaled = jnp.concatenate(scaled, 0)
    out_ref[...] = jnp.dot(kernel_ref[...], scaled, preferred_element_type=F32).astype(BF)


def first_product(parts, panel, kernel):
    return pl.pallas_call(
        first_kernel,
        out_shape=(
            jax.ShapeDtypeStruct((A, LANES), BF),
            jax.ShapeDtypeStruct((16, LANES), F32),
        ),
        compiler_params=PARAMS,
        cost_estimate=pl.CostEstimate(
            flops=2 * A * B * LANES, bytes_accessed=5 << 20, transcendentals=0
        ),
        name="first_product",
    )(parts, panel, kernel)


def second_kernel(scaled_ref, kernel_ref, out_ref):
    scaled = scaled_ref[...].reshape(B, LANES)
    out_ref[...] = jnp.dot(kernel_ref[...], scaled, preferred_element_type=F32).astype(BF)


def second_product(scaled, kernel):
    return pl.pallas_call(
        second_kernel,
        out_shape=jax.ShapeDtypeStruct((A, LANES), BF),
        compiler_params=PARAMS,
        cost_estimate=pl.CostEstimate(
            flops=2 * A * B * LANES, bytes_accessed=5 << 20, transcendentals=0
        ),
        name="second_product",
    )(scaled, kernel)


def per_device(embeddings, prior_scores, seed_labels, tile_pattern):
    z, xl = lax.axis_index("z"), lax.axis_index("xl")
    halves = [embeddings[:, :LANES], embeddings[:, LANES:]]

    flags = jnp.repeat(tile_pattern[:, 0].astype(BF), LANES // 2)
    flags = jnp.broadcast_to(flags[None, :], (8, LANES))
    other = lax.ppermute(flags, "xl", [(0, 1), (1, 0)])
    flags = [jnp.where(xl == 0, flags, other), jnp.where(xl == 0, other, flags)]

    panel = spread_gather(jnp.concatenate(halves + [prior_scores], 0), PLANE, 32)

    column = lax.all_gather(jnp.concatenate(halves + flags, 0), "z", axis=0)
    kept = column[:, 2 * N :: 8, :: LANES // 2]
    kept = lax.dynamic_index_in_dim(kept, z // 8, 1, False)
    offset = jnp.where(kept > 0, -RATE, DROPPED).astype(F32).reshape(8, 2, 2)
    offset = offset.transpose(2, 1, 0).reshape(2, 16)
    offset = jnp.broadcast_to(offset[..., None], (2, 16, LANES))

    kernel, sums = similarity(column, panel, offset)
    parts = spread_gather(sums, PLANE, 32)
    part, inv = first_product(parts, panel, kernel)
    inv_own = lax.dynamic_index_in_dim(inv.reshape(32, N), lax.axis_index(PLANE), 0, False)[:, None]
    classes_iota = jnp.arange(LANES, dtype=jnp.int32)
    seeds = SEED_WEIGHT * (seed_labels[:, None] == classes_iota[None, :]).astype(F32)

    part = lax.all_to_all(part.reshape(16, N, LANES), "z", 0, 0, tiled=True)
    product = jnp.sum(part.astype(F32), axis=0)
    scores = PROPAGATE_WEIGHT * inv_own * product + seeds

    scaled = spread_gather((inv_own * scores).astype(BF), PLANE[1:], 16)
    scaled = lax.all_gather(scaled, "core", axis=0)
    part = second_product(scaled, kernel)
    part = lax.all_to_all(part.reshape(16, N, LANES), "z", 0, 0, tiled=True)
    product = jnp.sum(part.astype(F32), axis=0)
    return PROPAGATE_WEIGHT * inv_own * product + seeds


def solution(mesh):
    return jax.shard_map(
        per_device,
        mesh=Mesh(mesh.devices.reshape(SIZES), AXES),
        in_specs=(P(AXES, None), P(AXES, None), P(AXES), P(ROW, COL)),
        out_specs=P(AXES, None),
        check_vma=False,
    )
```

```python
import jax
import jax.numpy as jnp
from jax import lax
from jax.experimental import pallas as pl
from jax.experimental.pallas import tpu as pltpu
from jax.sharding import Mesh, PartitionSpec as P

KERNEL_SPREAD = 0.05
PROPAGATE_WEIGHT = 0.9
SEED_WEIGHT = 0.1
RATE = 1.4426950408889634 / KERNEL_SPREAD
DROPPED = -1.0e30

AXES = ("xh", "y", "core", "z", "xl")
SIZES = (2, 4, 2, 16, 2)
ROW = ("xh", "y", "core")
COL = ("z", "xl")
LANES = 128
N = 64
A = 16 * N
B = 32 * N
PLANE = ("core", "xh", "y", "xl")
BF = jnp.bfloat16
F32 = jnp.float32
PARAMS = pltpu.CompilerParams(vmem_limit_bytes=24 * 1024 * 1024)


def spread_gather(x, axes, count):
    copies = jnp.broadcast_to(x[None], (count,) + x.shape)
    return lax.all_to_all(copies, axes, 0, 0, tiled=True)


def similarity_kernel(column_ref, panel_ref, offset_ref, kernel_ref, sums_ref):
    for j in range(8):
        lo = panel_ref[4 * j : 4 * j + 4, :N, :].reshape(4 * N, LANES)
        hi = panel_ref[4 * j : 4 * j + 4, N : 2 * N, :].reshape(4 * N, LANES)
        right = jnp.concatenate([lo, hi], 1)
        sums = jnp.zeros((1, 4 * N), F32)
        for a in range(2):
            offset = jnp.concatenate(
                [offset_ref[a, 2 * j : 2 * j + 1, :], offset_ref[a, 2 * j + 1 : 2 * j + 2, :]], 1
            )
            for q in range(2):
                rows = 4 * (2 * a + q)
                lo = column_ref[rows : rows + 4, :N, :].reshape(4 * N, LANES)
                hi = column_ref[rows : rows + 4, N : 2 * N, :].reshape(4 * N, LANES)
                left = jnp.concatenate([lo, hi], 1)
                weights = lax.dot_general(
                    left, right, (((1,), (1,)), ((), ())), preferred_element_type=F32
                )
                tile = jnp.exp2(weights * RATE + offset).astype(BF)
                kernel_ref[rows * N : (rows + 4) * N, 4 * j * N : 4 * (j + 1) * N] = tile
                sums = sums + jnp.sum(tile.astype(F32), axis=0, keepdims=True)
        sums_ref[2 * j : 2 * j + 1, :] = sums[:, :LANES]
        sums_ref[2 * j + 1 : 2 * j + 2, :] = sums[:, LANES:]


def similarity(column, panel, offset):
    return pl.pallas_call(
        similarity_kernel,
        out_shape=(jax.ShapeDtypeStruct((A, B), BF), jax.ShapeDtypeStruct((16, LANES), F32)),
        compiler_params=PARAMS,
        cost_estimate=pl.CostEstimate(
            flops=2 * A * B * 256, bytes_accessed=4 << 20, transcendentals=A * B
        ),
        name="similarity",
    )(column, panel, offset)


def first_kernel(parts_ref, panel_ref, kernel_ref, out_ref, inv_ref):
    inv = 1.0 / jnp.sqrt(jnp.sum(parts_ref[...], axis=0))
    inv_ref[...] = inv
    turned = inv.T
    scaled = []
    for k in range(16):
        prior = panel_ref[2 * k : 2 * k + 2, 2 * N : 3 * N, :].reshape(2 * N, LANES).astype(F32)
        scaled.append((turned[:, k : k + 1] * prior).astype(BF))
    scaled = jnp.concatenate(scaled, 0)
    out_ref[...] = jnp.dot(kernel_ref[...], scaled, preferred_element_type=F32).astype(BF)


def first_product(parts, panel, kernel):
    return pl.pallas_call(
        first_kernel,
        out_shape=(
            jax.ShapeDtypeStruct((A, LANES), BF),
            jax.ShapeDtypeStruct((16, LANES), F32),
        ),
        compiler_params=PARAMS,
        cost_estimate=pl.CostEstimate(
            flops=2 * A * B * LANES, bytes_accessed=5 << 20, transcendentals=0
        ),
        name="first_product",
    )(parts, panel, kernel)


def second_kernel(scaled_ref, kernel_ref, out_ref):
    scaled = scaled_ref[...].reshape(B, LANES)
    out_ref[...] = jnp.dot(kernel_ref[...], scaled, preferred_element_type=F32).astype(BF)


def second_product(scaled, kernel):
    return pl.pallas_call(
        second_kernel,
        out_shape=jax.ShapeDtypeStruct((A, LANES), BF),
        compiler_params=PARAMS,
        cost_estimate=pl.CostEstimate(
            flops=2 * A * B * LANES, bytes_accessed=5 << 20, transcendentals=0
        ),
        name="second_product",
    )(scaled, kernel)


def per_device(embeddings, prior_scores, seed_labels, tile_pattern):
    z, xl = lax.axis_index("z"), lax.axis_index("xl")
    halves = [embeddings[:, :LANES], embeddings[:, LANES:]]

    flags = jnp.repeat(tile_pattern[:, 0].astype(BF), LANES // 2)
    flags = jnp.broadcast_to(flags[None, :], (8, LANES))
    other = lax.ppermute(flags, "xl", [(0, 1), (1, 0)])
    flags = [jnp.where(xl == 0, flags, other), jnp.where(xl == 0, other, flags)]

    load = jnp.concatenate(halves + [prior_scores], 0)
    flags, load = lax.optimization_barrier((flags, load))
    panel = spread_gather(load, PLANE, 32)

    column = lax.all_gather(jnp.concatenate(halves + flags, 0), "z", axis=0)
    kept = column[:, 2 * N :: 8, :: LANES // 2]
    kept = lax.dynamic_index_in_dim(kept, z // 8, 1, False)
    offset = jnp.where(kept > 0, -RATE, DROPPED).astype(F32).reshape(8, 2, 2)
    offset = offset.transpose(2, 1, 0).reshape(2, 16)
    offset = jnp.broadcast_to(offset[..., None], (2, 16, LANES))

    kernel, sums = similarity(column, panel, offset)
    parts = spread_gather(sums, PLANE, 32)
    part, inv = first_product(parts, panel, kernel)
    inv_own = lax.dynamic_index_in_dim(inv.reshape(32, N), lax.axis_index(PLANE), 0, False)[:, None]
    classes_iota = jnp.arange(LANES, dtype=jnp.int32)
    seeds = SEED_WEIGHT * (seed_labels[:, None] == classes_iota[None, :]).astype(F32)

    part = lax.all_to_all(part.reshape(16, N, LANES), "z", 0, 0, tiled=True)
    product = jnp.sum(part.astype(F32), axis=0)
    scores = PROPAGATE_WEIGHT * inv_own * product + seeds

    scaled = spread_gather((inv_own * scores).astype(BF), PLANE[1:], 16)
    scaled = lax.all_gather(scaled, "core", axis=0)
    part = second_product(scaled, kernel)
    part = lax.all_to_all(part.reshape(16, N, LANES), "z", 0, 0, tiled=True)
    product = jnp.sum(part.astype(F32), axis=0)
    return PROPAGATE_WEIGHT * inv_own * product + seeds


def solution(mesh):
    return jax.shard_map(
        per_device,
        mesh=Mesh(mesh.devices.reshape(SIZES), AXES),
        in_specs=(P(AXES, None), P(AXES, None), P(AXES), P(ROW, COL)),
        out_specs=P(AXES, None),
        check_vma=False,
    )
```

```python
import jax
import jax.numpy as jnp
from jax import lax
from jax.experimental import pallas as pl
from jax.experimental.pallas import tpu as pltpu
from jax.sharding import Mesh, PartitionSpec as P

KERNEL_SPREAD = 0.05
PROPAGATE_WEIGHT = 0.9
SEED_WEIGHT = 0.1
RATE = 1.4426950408889634 / KERNEL_SPREAD
DROPPED = -1.0e30

AXES = ("xh", "y", "core", "z", "xl")
SIZES = (2, 4, 2, 16, 2)
ROW = ("xh", "y", "core")
COL = ("z", "xl")
LANES = 128
N = 64
A = 16 * N
B = 32 * N
PLANE = ("core", "xh", "y", "xl")
BF = jnp.bfloat16
F32 = jnp.float32
PARAMS = pltpu.CompilerParams(vmem_limit_bytes=24 * 1024 * 1024)


def spread_gather(x, axes, count):
    copies = jnp.broadcast_to(x[None], (count,) + x.shape)
    return lax.all_to_all(copies, axes, 0, 0, tiled=True)


def load_kernel(emb_ref, prior_ref, copies_ref, stacked_ref):
    emb = jnp.concatenate([emb_ref[:, :LANES], emb_ref[:, LANES:]], 0)
    stacked_ref[...] = emb
    rows = jnp.concatenate([emb, prior_ref[...]], 0)
    for i in range(32):
        copies_ref[i] = rows


def make_loads(embeddings, prior_scores):
    return pl.pallas_call(
        load_kernel,
        out_shape=(
            jax.ShapeDtypeStruct((32, 3 * N, LANES), BF),
            jax.ShapeDtypeStruct((2 * N, LANES), BF),
        ),
        compiler_params=PARAMS,
        cost_estimate=pl.CostEstimate(flops=0, bytes_accessed=4 << 20, transcendentals=0),
        name="make_loads",
    )(embeddings, prior_scores)


def similarity_kernel(half_ref, column_ref, panel_ref, kernel_ref, sums_ref):
    offsets = []
    for b in range(16):
        flags = column_ref[(b % 8) * 2 + b // 8, 2 * N :, :].astype(F32)
        flags = jnp.where(half_ref[0] == 0, flags[:8], flags[8:])
        offsets.append(jnp.where(flags > 0.5, -RATE, DROPPED))
    for j in range(8):
        lo = panel_ref[4 * j : 4 * j + 4, :N, :].reshape(4 * N, LANES)
        hi = panel_ref[4 * j : 4 * j + 4, N : 2 * N, :].reshape(4 * N, LANES)
        right = jnp.concatenate([lo, hi], 1)
        sums = jnp.zeros((1, 4 * N), F32)
        for a in range(2):
            row = slice(4 * a, 4 * a + 1)
            offset = jnp.concatenate([offsets[2 * j][row], offsets[2 * j + 1][row]], 1)
            for q in range(2):
                rows = 4 * (2 * a + q)
                lo = column_ref[rows : rows + 4, :N, :].reshape(4 * N, LANES)
                hi = column_ref[rows : rows + 4, N : 2 * N, :].reshape(4 * N, LANES)
                left = jnp.concatenate([lo, hi], 1)
                weights = lax.dot_general(
                    left, right, (((1,), (1,)), ((), ())), preferred_element_type=F32
                )
                tile = jnp.exp2(weights * RATE + offset).astype(BF)
                kernel_ref[rows * N : (rows + 4) * N, 4 * j * N : 4 * (j + 1) * N] = tile
                sums = sums + jnp.sum(tile.astype(F32), axis=0, keepdims=True)
        sums_ref[2 * j : 2 * j + 1, :] = sums[:, :LANES]
        sums_ref[2 * j + 1 : 2 * j + 2, :] = sums[:, LANES:]


def similarity(half, column, panel):
    vmem = pl.BlockSpec(memory_space=pltpu.VMEM)
    return pl.pallas_call(
        similarity_kernel,
        in_specs=[pl.BlockSpec(memory_space=pltpu.SMEM), vmem, vmem],
        out_shape=(jax.ShapeDtypeStruct((A, B), BF), jax.ShapeDtypeStruct((16, LANES), F32)),
        compiler_params=PARAMS,
        cost_estimate=pl.CostEstimate(
            flops=2 * A * B * 256, bytes_accessed=4 << 20, transcendentals=A * B
        ),
        name="similarity",
    )(half, column, panel)


def first_kernel(parts_ref, panel_ref, kernel_ref, out_ref, inv_ref):
    inv = 1.0 / jnp.sqrt(jnp.sum(parts_ref[...], axis=0))
    inv_ref[...] = inv
    turned = inv.T
    scaled = []
    for k in range(16):
        prior = panel_ref[2 * k : 2 * k + 2, 2 * N : 3 * N, :].reshape(2 * N, LANES).astype(F32)
        scaled.append((turned[:, k : k + 1] * prior).astype(BF))
    scaled = jnp.concatenate(scaled, 0)
    out_ref[...] = jnp.dot(kernel_ref[...], scaled, preferred_element_type=F32).astype(BF)


def first_product(parts, panel, kernel):
    return pl.pallas_call(
        first_kernel,
        out_shape=(
            jax.ShapeDtypeStruct((A, LANES), BF),
            jax.ShapeDtypeStruct((16, LANES), F32),
        ),
        compiler_params=PARAMS,
        cost_estimate=pl.CostEstimate(
            flops=2 * A * B * LANES, bytes_accessed=5 << 20, transcendentals=0
        ),
        name="first_product",
    )(parts, panel, kernel)


PIECES = 8
ROWS = A // PIECES


def second_kernel(scaled_ref, kernel_ref, out_ref, held, sems):
    copies = [
        pltpu.make_async_copy(
            kernel_ref.at[pl.ds(i * ROWS, ROWS)], held.at[pl.ds(i * ROWS, ROWS)], sems.at[i]
        )
        for i in range(PIECES)
    ]
    for copy in copies:
        copy.start()
    scaled = scaled_ref[...].reshape(B, LANES)
    for i, copy in enumerate(copies):
        copy.wait()
        rows = slice(i * ROWS, (i + 1) * ROWS)
        out_ref[rows] = jnp.dot(held[rows], scaled, preferred_element_type=F32).astype(BF)


def second_product(scaled, kernel):
    return pl.pallas_call(
        second_kernel,
        in_specs=[
            pl.BlockSpec(memory_space=pltpu.VMEM),
            pl.BlockSpec(memory_space=pltpu.HBM),
        ],
        out_shape=jax.ShapeDtypeStruct((A, LANES), BF),
        scratch_shapes=[pltpu.VMEM((A, B), BF), pltpu.SemaphoreType.DMA((PIECES,))],
        compiler_params=pltpu.CompilerParams(vmem_limit_bytes=60 * 1024 * 1024),
        cost_estimate=pl.CostEstimate(
            flops=2 * A * B * LANES, bytes_accessed=5 << 20, transcendentals=0
        ),
        name="second_product",
    )(scaled, kernel)


def per_device(embeddings, prior_scores, seed_labels, tile_pattern):
    z, xl = lax.axis_index("z"), lax.axis_index("xl")
    loads, stacked = make_loads(embeddings, prior_scores)

    flags = jnp.repeat(tile_pattern.astype(BF), 4, axis=0)
    flags = jnp.broadcast_to(flags, (8, LANES))
    other = lax.ppermute(flags, "xl", [(0, 1), (1, 0)])
    flags = [jnp.where(xl == 0, flags, other), jnp.where(xl == 0, other, flags)]

    flags, loads = lax.optimization_barrier((flags, loads))
    panel = lax.all_to_all(loads, PLANE, 0, 0, tiled=True)

    column = lax.all_gather(jnp.concatenate([stacked] + flags, 0), "z", axis=0)
    half = (z // 8).astype(jnp.int32).reshape(1)
    kernel, sums = similarity(half, column, panel)
    parts = spread_gather(sums, PLANE, 32)
    part, inv = first_product(parts, panel, kernel)
    inv_own = lax.dynamic_index_in_dim(inv.reshape(32, N), lax.axis_index(PLANE), 0, False)[:, None]
    classes_iota = jnp.arange(LANES, dtype=jnp.int32)
    seeds = SEED_WEIGHT * (seed_labels[:, None] == classes_iota[None, :]).astype(F32)

    part = lax.all_to_all(part.reshape(16, N, LANES), "z", 0, 0, tiled=True)
    product = jnp.sum(part.astype(F32), axis=0)
    scores = PROPAGATE_WEIGHT * inv_own * product + seeds

    scaled = spread_gather((inv_own * scores).astype(BF), PLANE[1:], 16)
    scaled = lax.all_gather(scaled, "core", axis=0)
    part = second_product(scaled, kernel)
    part = lax.all_to_all(part.reshape(16, N, LANES), "z", 0, 0, tiled=True)
    product = jnp.sum(part.astype(F32), axis=0)
    return PROPAGATE_WEIGHT * inv_own * product + seeds


def solution(mesh):
    return jax.shard_map(
        per_device,
        mesh=Mesh(mesh.devices.reshape(SIZES), AXES),
        in_specs=(P(AXES, None), P(AXES, None), P(AXES), P(ROW, COL)),
        out_specs=P(AXES, None),
        check_vma=False,
    )
```

```python
import jax
import jax.numpy as jnp
from jax import lax
from jax.experimental import pallas as pl
from jax.experimental.pallas import tpu as pltpu
from jax.sharding import Mesh, PartitionSpec as P

KERNEL_SPREAD = 0.05
PROPAGATE_WEIGHT = 0.9
SEED_WEIGHT = 0.1
RATE = 1.4426950408889634 / KERNEL_SPREAD
DROPPED = -1.0e30

AXES = ("xh", "y", "core", "z", "xl")
SIZES = (2, 4, 2, 16, 2)
ROW = ("xh", "y", "core")
COL = ("z", "xl")
LANES = 128
N = 64
A = 16 * N
B = 32 * N
PLANE = ("core", "xh", "y", "xl")
PIECES = 4
DEPTH = B // PIECES
BF = jnp.bfloat16
F32 = jnp.float32
PARAMS = pltpu.CompilerParams(vmem_limit_bytes=24 * 1024 * 1024)


def spread_gather(x, axes, count):
    copies = jnp.broadcast_to(x[None], (count,) + x.shape)
    return lax.all_to_all(copies, axes, 0, 0, tiled=True)


def load_kernel(emb_ref, copies_ref, stacked_ref):
    emb = jnp.concatenate([emb_ref[:, :LANES], emb_ref[:, LANES:]], 0)
    stacked_ref[...] = emb
    for i in range(32):
        copies_ref[i] = emb


def make_loads(embeddings):
    return pl.pallas_call(
        load_kernel,
        out_shape=(
            jax.ShapeDtypeStruct((32, 2 * N, LANES), BF),
            jax.ShapeDtypeStruct((2 * N, LANES), BF),
        ),
        compiler_params=PARAMS,
        cost_estimate=pl.CostEstimate(flops=0, bytes_accessed=4 << 20, transcendentals=0),
        name="make_loads",
    )(embeddings)


def rows_of(ref, i):
    lo = ref[4 * i : 4 * i + 4, :N, :].reshape(4 * N, LANES)
    hi = ref[4 * i : 4 * i + 4, N : 2 * N, :].reshape(4 * N, LANES)
    return jnp.concatenate([lo, hi], 1)


def weigh(left, right):
    return lax.dot_general(left, right, (((1,), (1,)), ((), ())), preferred_element_type=F32) * RATE


def mask_offsets(half_ref, column_ref):
    offsets = []
    for b in range(16):
        flags = column_ref[(b % 8) * 2 + b // 8, 3 * N :, :].astype(F32)
        flags = jnp.where(half_ref[0] == 0, flags[:8], flags[8:])
        offsets.append(jnp.where(flags > 0.5, -RATE, DROPPED))
    return offsets


def first_block_kernel(half_ref, column_ref, panel_ref, kernel_ref, sums_ref):
    offsets = mask_offsets(half_ref, column_ref)
    for j in range(4):
        right = rows_of(column_ref, j)
        row = slice(4 * (j // 2), 4 * (j // 2) + 1)
        sums = jnp.zeros((1, 4 * N), F32)
        for i in range(8):
            weights = weigh(rows_of(panel_ref, i), right)
            for k in range(2):
                offset = offsets[2 * i + k][row]
                offset = jnp.concatenate([offset, offset], 1)
                tile = jnp.exp2(weights[2 * N * k : 2 * N * (k + 1)] + offset).astype(BF)
                top = 4 * N * i + 2 * N * k
                kernel_ref[top : top + 2 * N, 4 * N * j : 4 * N * (j + 1)] = tile
                sums = sums + jnp.sum(tile.astype(F32), axis=0, keepdims=True)
        sums_ref[2 * j : 2 * j + 1, :] = sums[:, :LANES]
        sums_ref[2 * j + 1 : 2 * j + 2, :] = sums[:, LANES:]


def second_block_kernel(half_ref, column_ref, panel_ref, *kernel_refs):
    offsets = mask_offsets(half_ref, column_ref)
    for j in range(8):
        right = rows_of(panel_ref, j)
        for i in range(4):
            row = slice(4 * (i // 2), 4 * (i // 2) + 1)
            offset = jnp.concatenate([offsets[2 * j][row], offsets[2 * j + 1][row]], 1)
            tile = jnp.exp2(weigh(rows_of(column_ref, i), right) + offset).astype(BF)
            at = 4 * N * j % DEPTH
            kernel_refs[4 * N * j // DEPTH][4 * N * i : 4 * N * (i + 1), at : at + 4 * N] = tile


def make_block(body, out_shape, name, half, column, panel):
    vmem = pl.BlockSpec(memory_space=pltpu.VMEM)
    return pl.pallas_call(
        body,
        in_specs=[pl.BlockSpec(memory_space=pltpu.SMEM), vmem, vmem],
        out_shape=out_shape,
        compiler_params=PARAMS,
        cost_estimate=pl.CostEstimate(
            flops=2 * A * B * 256, bytes_accessed=4 << 20, transcendentals=A * B
        ),
        name=name,
    )(half, column, panel)


def first_kernel(parts_ref, column_ref, kernel_ref, out_ref, inv_ref):
    inv = 1.0 / jnp.sqrt(jnp.sum(parts_ref[...], axis=0))
    inv_ref[...] = inv
    turned = inv.T
    scaled = []
    for k in range(8):
        prior = column_ref[2 * k : 2 * k + 2, 2 * N : 3 * N, :].reshape(2 * N, LANES).astype(F32)
        scaled.append((turned[:, k : k + 1] * prior).astype(BF))
    scaled = jnp.concatenate(scaled, 0)
    out_ref[...] = jnp.dot(kernel_ref[...], scaled, preferred_element_type=F32).astype(BF)


def first_product(parts, column, kernel):
    return pl.pallas_call(
        first_kernel,
        out_shape=(
            jax.ShapeDtypeStruct((B, LANES), BF),
            jax.ShapeDtypeStruct((8, LANES), F32),
        ),
        compiler_params=PARAMS,
        cost_estimate=pl.CostEstimate(
            flops=2 * A * B * LANES, bytes_accessed=5 << 20, transcendentals=0
        ),
        name="first_product",
    )(parts, column, kernel)


def second_kernel(scaled_ref, *refs):
    kernel_refs, out_ref = refs[:PIECES], refs[PIECES]
    shards = DEPTH // N
    total = None
    for i, kernel_ref in enumerate(kernel_refs):
        first = i * shards
        scaled = scaled_ref[first // 16, first % 16 : first % 16 + shards].reshape(DEPTH, LANES)
        part = jnp.dot(kernel_ref[...], scaled, preferred_element_type=F32)
        total = part if total is None else total + part
    out_ref[...] = total.astype(BF)


def second_product(scaled, blocks):
    return pl.pallas_call(
        second_kernel,
        out_shape=jax.ShapeDtypeStruct((A, LANES), BF),
        compiler_params=PARAMS,
        cost_estimate=pl.CostEstimate(
            flops=2 * A * B * LANES, bytes_accessed=5 << 20, transcendentals=0
        ),
        name="second_product",
    )(scaled, *blocks)


def per_device(embeddings, prior_scores, seed_labels, tile_pattern):
    z, xl = lax.axis_index("z"), lax.axis_index("xl")
    half = (z // 8).astype(jnp.int32).reshape(1)
    loads, stacked = make_loads(embeddings)

    flags = jnp.repeat(tile_pattern.astype(BF), 4, axis=0)
    flags = jnp.broadcast_to(flags, (8, LANES))
    other = lax.ppermute(flags, "xl", [(0, 1), (1, 0)])
    flags = [jnp.where(xl == 0, flags, other), jnp.where(xl == 0, other, flags)]

    flags, loads = lax.optimization_barrier((flags, loads))
    panel = lax.all_to_all(loads, PLANE, 0, 0, tiled=True)

    column = lax.all_gather(jnp.concatenate([stacked, prior_scores] + flags, 0), "z", axis=0)

    block_ba, sums = make_block(
        first_block_kernel,
        (jax.ShapeDtypeStruct((B, A), BF), jax.ShapeDtypeStruct((8, LANES), F32)),
        "block_ba",
        half,
        column,
        panel,
    )
    parts = spread_gather(sums, "z", 16)
    part, inv = first_product(parts, column, block_ba)
    inv_own = lax.dynamic_index_in_dim(inv.reshape(16, N), z, 0, False)[:, None]
    classes_iota = jnp.arange(LANES, dtype=jnp.int32)
    seeds = SEED_WEIGHT * (seed_labels[:, None] == classes_iota[None, :]).astype(F32)

    part = lax.all_to_all(part.reshape(32, N, LANES), PLANE, 0, 0, tiled=True)
    product = jnp.sum(part.astype(F32), axis=0)
    scores = PROPAGATE_WEIGHT * inv_own * product + seeds

    scaled = (inv_own * scores).astype(BF)
    scaled, column = lax.optimization_barrier((scaled, column))
    scaled = spread_gather(scaled, PLANE[1:], 16)
    piece = jax.ShapeDtypeStruct((A, DEPTH), BF)
    block_ab = make_block(second_block_kernel, (piece,) * PIECES, "block_ab", half, column, panel)
    scaled = lax.all_gather(scaled, "core", axis=0)
    part = second_product(scaled, block_ab)
    part = lax.all_to_all(part.reshape(16, N, LANES), "z", 0, 0, tiled=True)
    product = jnp.sum(part.astype(F32), axis=0)
    return PROPAGATE_WEIGHT * inv_own * product + seeds


def solution(mesh):
    return jax.shard_map(
        per_device,
        mesh=Mesh(mesh.devices.reshape(SIZES), AXES),
        in_specs=(P(AXES, None), P(AXES, None), P(AXES), P(ROW, COL)),
        out_specs=P(AXES, None),
        check_vma=False,
    )
```

```python
import jax
import jax.numpy as jnp
from jax import lax
from jax.experimental import pallas as pl
from jax.experimental.pallas import tpu as pltpu
from jax.sharding import Mesh, PartitionSpec as P

KERNEL_SPREAD = 0.05
PROPAGATE_WEIGHT = 0.9
SEED_WEIGHT = 0.1
RATE = 1.4426950408889634 / KERNEL_SPREAD
DROPPED = -1.0e30

AXES = ("xh", "y", "core", "z", "xl")
SIZES = (2, 4, 2, 16, 2)
ROW = ("xh", "y", "core")
COL = ("z", "xl")
LANES = 128
N = 64
A = 16 * N
B = 32 * N
PLANE = ("core", "xh", "y", "xl")
BF = jnp.bfloat16
F32 = jnp.float32
PARAMS = pltpu.CompilerParams(vmem_limit_bytes=24 * 1024 * 1024)


def spread_gather(x, axes, count):
    copies = jnp.broadcast_to(x[None], (count,) + x.shape)
    return lax.all_to_all(copies, axes, 0, 0, tiled=True)


def load_kernel(emb_ref, prior_ref, copies_ref, stacked_ref):
    emb = jnp.concatenate([emb_ref[:, :LANES], emb_ref[:, LANES:]], 0)
    stacked_ref[: 2 * N] = emb
    stacked_ref[2 * N :] = prior_ref[...]
    for i in range(32):
        copies_ref[i] = emb


def make_loads(embeddings, prior_scores):
    return pl.pallas_call(
        load_kernel,
        out_shape=(
            jax.ShapeDtypeStruct((32, 2 * N, LANES), BF),
            jax.ShapeDtypeStruct((3 * N, LANES), BF),
        ),
        compiler_params=PARAMS,
        cost_estimate=pl.CostEstimate(flops=0, bytes_accessed=4 << 20, transcendentals=0),
        name="make_loads",
    )(embeddings, prior_scores)


def rows_of(ref, i):
    lo = ref[4 * i : 4 * i + 4, :N, :].reshape(4 * N, LANES)
    hi = ref[4 * i : 4 * i + 4, N : 2 * N, :].reshape(4 * N, LANES)
    return jnp.concatenate([lo, hi], 1)


def weigh(left, right):
    return lax.dot_general(left, right, (((1,), (1,)), ((), ())), preferred_element_type=F32) * RATE


def mask_offsets(half_ref, column_ref):
    offsets = []
    for b in range(16):
        flags = column_ref[(b % 8) * 2 + b // 8, 3 * N :, :].astype(F32)
        flags = jnp.where(half_ref[0] == 0, flags[:8], flags[8:])
        offsets.append(jnp.where(flags > 0.5, -RATE, DROPPED))
    return offsets


def first_block_kernel(half_ref, column_ref, panel_ref, kernel_ref, sums_ref):
    offsets = mask_offsets(half_ref, column_ref)
    for j in range(4):
        right = rows_of(column_ref, j)
        row = slice(4 * (j // 2), 4 * (j // 2) + 1)
        sums = jnp.zeros((1, 4 * N), F32)
        for i in range(8):
            weights = weigh(rows_of(panel_ref, i), right)
            for k in range(2):
                offset = offsets[2 * i + k][row]
                offset = jnp.concatenate([offset, offset], 1)
                tile = jnp.exp2(weights[2 * N * k : 2 * N * (k + 1)] + offset).astype(BF)
                top = 4 * N * i + 2 * N * k
                kernel_ref[top : top + 2 * N, 4 * N * j : 4 * N * (j + 1)] = tile
                sums = sums + jnp.sum(tile.astype(F32), axis=0, keepdims=True)
        sums_ref[2 * j : 2 * j + 1, :] = sums[:, :LANES]
        sums_ref[2 * j + 1 : 2 * j + 2, :] = sums[:, LANES:]


def first_block(half, column, panel):
    vmem = pl.BlockSpec(memory_space=pltpu.VMEM)
    return pl.pallas_call(
        first_block_kernel,
        in_specs=[pl.BlockSpec(memory_space=pltpu.SMEM), vmem, vmem],
        out_shape=(jax.ShapeDtypeStruct((B, A), BF), jax.ShapeDtypeStruct((8, LANES), F32)),
        compiler_params=PARAMS,
        cost_estimate=pl.CostEstimate(
            flops=2 * A * B * 256, bytes_accessed=4 << 20, transcendentals=A * B
        ),
        name="first_block",
    )(half, column, panel)


def first_kernel(parts_ref, column_ref, kernel_ref, out_ref, inv_ref):
    inv = 1.0 / jnp.sqrt(jnp.sum(parts_ref[...], axis=0))
    inv_ref[...] = inv
    turned = inv.T
    scaled = []
    for k in range(8):
        prior = column_ref[2 * k : 2 * k + 2, 2 * N : 3 * N, :].reshape(2 * N, LANES).astype(F32)
        scaled.append((turned[:, k : k + 1] * prior).astype(BF))
    scaled = jnp.concatenate(scaled, 0)
    out_ref[...] = jnp.dot(kernel_ref[...], scaled, preferred_element_type=F32).astype(BF)


def first_product(parts, column, kernel):
    return pl.pallas_call(
        first_kernel,
        out_shape=(
            jax.ShapeDtypeStruct((B, LANES), BF),
            jax.ShapeDtypeStruct((8, LANES), F32),
        ),
        compiler_params=PARAMS,
        cost_estimate=pl.CostEstimate(
            flops=2 * A * B * LANES, bytes_accessed=5 << 20, transcendentals=0
        ),
        name="first_product",
    )(parts, column, kernel)


def second_kernel(half_ref, column_ref, panel_ref, scaled_ref, out_ref):
    offsets = mask_offsets(half_ref, column_ref)
    for i in range(4):
        row = slice(4 * (i // 2), 4 * (i // 2) + 1)
        left = rows_of(column_ref, i)
        total = jnp.zeros((4 * N, LANES), F32)
        for j in range(8):
            offset = jnp.concatenate([offsets[2 * j][row], offsets[2 * j + 1][row]], 1)
            tile = jnp.exp2(weigh(left, rows_of(panel_ref, j)) + offset).astype(BF)
            at = 4 * j % 16
            scaled = scaled_ref[j // 4, at : at + 4].reshape(4 * N, LANES)
            total = total + jnp.dot(tile, scaled, preferred_element_type=F32)
        out_ref[4 * N * i : 4 * N * (i + 1)] = total.astype(BF)


def second_product(half, column, panel, scaled):
    vmem = pl.BlockSpec(memory_space=pltpu.VMEM)
    return pl.pallas_call(
        second_kernel,
        in_specs=[pl.BlockSpec(memory_space=pltpu.SMEM), vmem, vmem, vmem],
        out_shape=jax.ShapeDtypeStruct((A, LANES), BF),
        compiler_params=PARAMS,
        cost_estimate=pl.CostEstimate(
            flops=2 * A * B * (256 + LANES), bytes_accessed=3 << 20, transcendentals=A * B
        ),
        name="second_product",
    )(half, column, panel, scaled)


def per_device(embeddings, prior_scores, seed_labels, tile_pattern):
    z, xl = lax.axis_index("z"), lax.axis_index("xl")
    half = (z // 8).astype(jnp.int32).reshape(1)
    loads, stacked = make_loads(embeddings, prior_scores)

    flags = jnp.repeat(tile_pattern.astype(BF), 4, axis=0)
    flags = jnp.broadcast_to(flags, (8, LANES))
    other = lax.ppermute(flags, "xl", [(0, 1), (1, 0)])
    flags = [jnp.where(xl == 0, flags, other), jnp.where(xl == 0, other, flags)]

    flags, loads = lax.optimization_barrier((flags, loads))
    panel = lax.all_to_all(loads, PLANE, 0, 0, tiled=True)

    column = lax.all_gather(jnp.concatenate([stacked] + flags, 0), "z", axis=0)

    block, sums = first_block(half, column, panel)
    parts = spread_gather(sums, "z", 16)
    part, inv = first_product(parts, column, block)
    inv_own = lax.dynamic_index_in_dim(inv.reshape(16, N), z, 0, False)[:, None]
    classes_iota = jnp.arange(LANES, dtype=jnp.int32)
    seeds = SEED_WEIGHT * (seed_labels[:, None] == classes_iota[None, :]).astype(F32)

    part = lax.all_to_all(part.reshape(32, N, LANES), PLANE, 0, 0, tiled=True)
    product = jnp.sum(part.astype(F32), axis=0)
    scores = PROPAGATE_WEIGHT * inv_own * product + seeds

    scaled = spread_gather((inv_own * scores).astype(BF), PLANE[1:], 16)
    scaled = lax.all_gather(scaled, "core", axis=0)
    part = second_product(half, column, panel, scaled)
    part = lax.all_to_all(part.reshape(16, N, LANES), "z", 0, 0, tiled=True)
    product = jnp.sum(part.astype(F32), axis=0)
    return PROPAGATE_WEIGHT * inv_own * product + seeds


def solution(mesh):
    return jax.shard_map(
        per_device,
        mesh=Mesh(mesh.devices.reshape(SIZES), AXES),
        in_specs=(P(AXES, None), P(AXES, None), P(AXES), P(ROW, COL)),
        out_specs=P(AXES, None),
        check_vma=False,
    )
```

```python
import jax
import jax.numpy as jnp
from jax import lax
from jax.experimental import pallas as pl
from jax.experimental.pallas import tpu as pltpu
from jax.sharding import Mesh, PartitionSpec as P

KERNEL_SPREAD = 0.05
PROPAGATE_WEIGHT = 0.9
SEED_WEIGHT = 0.1
RATE = 1.4426950408889634 / KERNEL_SPREAD
DROPPED = -1.0e30

AXES = ("xh", "y", "core", "z", "xl")
SIZES = (2, 4, 2, 16, 2)
ROW = ("xh", "y", "core")
COL = ("z", "xl")
LANES = 128
N = 64
A = 16 * N
B = 32 * N
PLANE = ("core", "xh", "y", "xl")
BF = jnp.bfloat16
F32 = jnp.float32
PARAMS = pltpu.CompilerParams(vmem_limit_bytes=24 * 1024 * 1024)


def spread_gather(x, axes, count):
    copies = jnp.broadcast_to(x[None], (count,) + x.shape)
    return lax.all_to_all(copies, axes, 0, 0, tiled=True)


def load_kernel(emb_ref, prior_ref, copies_ref, stacked_ref):
    emb = jnp.concatenate([emb_ref[:, :LANES], emb_ref[:, LANES:]], 0)
    stacked_ref[: 2 * N] = emb
    stacked_ref[2 * N :] = prior_ref[...]
    for i in range(32):
        copies_ref[i] = emb


def make_loads(embeddings, prior_scores):
    return pl.pallas_call(
        load_kernel,
        out_shape=(
            jax.ShapeDtypeStruct((32, 2 * N, LANES), BF),
            jax.ShapeDtypeStruct((3 * N, LANES), BF),
        ),
        compiler_params=PARAMS,
        cost_estimate=pl.CostEstimate(flops=0, bytes_accessed=4 << 20, transcendentals=0),
        name="make_loads",
    )(embeddings, prior_scores)


def rows_of(ref, i):
    lo = ref[4 * i : 4 * i + 4, :N, :].reshape(4 * N, LANES)
    hi = ref[4 * i : 4 * i + 4, N : 2 * N, :].reshape(4 * N, LANES)
    return jnp.concatenate([lo, hi], 1)


def weigh(left, right):
    return lax.dot_general(left, right, (((1,), (1,)), ((), ())), preferred_element_type=F32) * RATE


def mask_offsets(half_ref, column_ref):
    offsets = []
    for b in range(16):
        flags = column_ref[(b % 8) * 2 + b // 8, 3 * N :, :].astype(F32)
        flags = jnp.where(half_ref[0] == 0, flags[:8], flags[8:])
        offsets.append(jnp.where(flags > 0.5, -RATE, DROPPED))
    return offsets


def first_block_kernel(half_ref, column_ref, panel_ref, kernel_ref, sums_ref):
    offsets = mask_offsets(half_ref, column_ref)
    for j in range(4):
        right = rows_of(column_ref, j)
        row = slice(4 * (j // 2), 4 * (j // 2) + 1)
        sums = jnp.zeros((8, 4 * N), F32)
        for i in range(8):
            weights = weigh(rows_of(panel_ref, i), right)
            for k in range(2):
                offset = offsets[2 * i + k][row]
                offset = jnp.concatenate([offset, offset], 1)
                tile = jnp.exp2(weights[2 * N * k : 2 * N * (k + 1)] + offset).astype(BF)
                top = 4 * N * i + 2 * N * k
                kernel_ref[top : top + 2 * N, 4 * N * j : 4 * N * (j + 1)] = tile
                sums = sums + jnp.sum(tile.astype(F32).reshape(N // 4, 8, 4 * N), axis=0)
        sums = jnp.sum(sums, axis=0, keepdims=True)
        sums_ref[2 * j : 2 * j + 1, :] = sums[:, :LANES]
        sums_ref[2 * j + 1 : 2 * j + 2, :] = sums[:, LANES:]


def first_block(half, column, panel):
    vmem = pl.BlockSpec(memory_space=pltpu.VMEM)
    return pl.pallas_call(
        first_block_kernel,
        in_specs=[pl.BlockSpec(memory_space=pltpu.SMEM), vmem, vmem],
        out_shape=(jax.ShapeDtypeStruct((B, A), BF), jax.ShapeDtypeStruct((8, LANES), F32)),
        compiler_params=PARAMS,
        cost_estimate=pl.CostEstimate(
            flops=2 * A * B * 256, bytes_accessed=4 << 20, transcendentals=A * B
        ),
        name="first_block",
    )(half, column, panel)


def first_kernel(z_ref, parts_ref, column_ref, kernel_ref, out_ref, own_ref):
    turned = (1.0 / jnp.sqrt(jnp.sum(parts_ref[...], axis=0))).T
    z = z_ref[0]
    own = jnp.zeros((N, LANES), F32)
    scaled = []
    for k in range(8):
        inv = jnp.broadcast_to(turned[:, k : k + 1], (2 * N, LANES))
        own = jnp.where(z == 2 * k, inv[:N], jnp.where(z == 2 * k + 1, inv[N:], own))
        prior = column_ref[2 * k : 2 * k + 2, 2 * N : 3 * N, :].reshape(2 * N, LANES).astype(F32)
        scaled.append((inv * prior).astype(BF))
    own_ref[...] = own
    scaled = jnp.concatenate(scaled, 0)
    out_ref[...] = jnp.dot(kernel_ref[...], scaled, preferred_element_type=F32).astype(BF)


def first_product(z, parts, column, kernel):
    vmem = pl.BlockSpec(memory_space=pltpu.VMEM)
    return pl.pallas_call(
        first_kernel,
        in_specs=[pl.BlockSpec(memory_space=pltpu.SMEM), vmem, vmem, vmem],
        out_shape=(
            jax.ShapeDtypeStruct((B, LANES), BF),
            jax.ShapeDtypeStruct((N, LANES), F32),
        ),
        compiler_params=PARAMS,
        cost_estimate=pl.CostEstimate(
            flops=2 * A * B * LANES, bytes_accessed=5 << 20, transcendentals=0
        ),
        name="first_product",
    )(z, parts, column, kernel)


def second_kernel(half_ref, column_ref, panel_ref, scaled_ref, out_ref, stripe_ref):
    offsets = mask_offsets(half_ref, column_ref)
    scaled = scaled_ref[...].reshape(B, LANES)
    for a in range(2):
        row = slice(4 * a, 4 * a + 1)
        for j in range(8):
            right = rows_of(panel_ref, j)
            offset = jnp.concatenate([offsets[2 * j][row], offsets[2 * j + 1][row]], 1)
            for i in range(2):
                tile = jnp.exp2(weigh(rows_of(column_ref, 2 * a + i), right) + offset).astype(BF)
                stripe_ref[a, 4 * N * i : 4 * N * (i + 1), 4 * N * j : 4 * N * (j + 1)] = tile
        part = jnp.dot(stripe_ref[a], scaled, preferred_element_type=F32)
        out_ref[8 * N * a : 8 * N * (a + 1)] = part.astype(BF)


def second_product(half, column, panel, scaled):
    vmem = pl.BlockSpec(memory_space=pltpu.VMEM)
    return pl.pallas_call(
        second_kernel,
        in_specs=[pl.BlockSpec(memory_space=pltpu.SMEM), vmem, vmem, vmem],
        out_shape=jax.ShapeDtypeStruct((A, LANES), BF),
        scratch_shapes=[pltpu.VMEM((2, A // 2, B), BF)],
        compiler_params=PARAMS,
        cost_estimate=pl.CostEstimate(
            flops=2 * A * B * (256 + LANES), bytes_accessed=3 << 20, transcendentals=A * B
        ),
        name="second_product",
    )(half, column, panel, scaled)


def per_device(embeddings, prior_scores, seed_labels, tile_pattern):
    z, xl = lax.axis_index("z"), lax.axis_index("xl")
    half = (z // 8).astype(jnp.int32).reshape(1)
    loads, stacked = make_loads(embeddings, prior_scores)

    flags = jnp.repeat(tile_pattern.astype(BF), 4, axis=0)
    flags = jnp.broadcast_to(flags, (8, LANES))
    other = lax.ppermute(flags, "xl", [(0, 1), (1, 0)])
    flags = [jnp.where(xl == 0, flags, other), jnp.where(xl == 0, other, flags)]

    flags, loads = lax.optimization_barrier((flags, loads))
    panel = lax.all_to_all(loads, PLANE, 0, 0, tiled=True)

    column = lax.all_gather(jnp.concatenate([stacked] + flags, 0), "z", axis=0)

    block, sums = first_block(half, column, panel)
    parts = spread_gather(sums, "z", 16)
    part, inv_own = first_product(z.astype(jnp.int32).reshape(1), parts, column, block)
    classes_iota = jnp.arange(LANES, dtype=jnp.int32)
    seeds = SEED_WEIGHT * (seed_labels[:, None] == classes_iota[None, :]).astype(F32)

    part = lax.all_to_all(part.reshape(32, N, LANES), PLANE, 0, 0, tiled=True)
    product = jnp.sum(part.astype(F32), axis=0)
    scores = PROPAGATE_WEIGHT * inv_own * product + seeds

    scaled = spread_gather((inv_own * scores).astype(BF), PLANE[1:], 16)
    scaled = lax.all_gather(scaled, "core", axis=0)
    part = second_product(half, column, panel, scaled)
    part = lax.all_to_all(part.reshape(16, N, LANES), "z", 0, 0, tiled=True)
    product = jnp.sum(part.astype(F32), axis=0)
    return PROPAGATE_WEIGHT * inv_own * product + seeds


def solution(mesh):
    return jax.shard_map(
        per_device,
        mesh=Mesh(mesh.devices.reshape(SIZES), AXES),
        in_specs=(P(AXES, None), P(AXES, None), P(AXES), P(ROW, COL)),
        out_specs=P(AXES, None),
        check_vma=False,
    )
```
